256 devices in a mesh: feat: 4 (over x), graph: 16 (over z, core), dp: 4 (over y).
Axes of the slice: x: 4, y: 4, z: 8, core: 2. Of those that a mesh axis runs over, the one named last changes fastest.
Arguments:
- features: bfloat16 [4, 32768, 768], P('dp', 'graph', 'feat'), may hold values from -6 to 6
- w1_self: bfloat16 [768, 1024], P('feat'), may hold values from -0.21875 to 0.21875
- w1_neigh: bfloat16 [768, 1024], P('feat'), may hold values from -0.625 to 0.625
- w2_self: bfloat16 [1024, 153], P('feat'), may hold values from -0.1875 to 0.1875
- w2_neigh: bfloat16 [1024, 153], P('feat'), may hold values from -0.5 to 0.5
- tile_rows: int32 [4, 16, 16, 3], P('dp', 'graph'), may hold values from 0 to 11, as said below
- tile_cols: int32 [4, 16, 16, 3], P('dp', 'graph'), may hold values from 0 to 15, as said below
- tile_count: int32 [4, 16, 16], P('dp', 'graph'), may hold values from 0 to 3, as said below
- tile_bits: int32 [4, 16, 16, 3, 128, 128], P('dp', 'graph'), may hold values 0 or 1
- d_logits: bfloat16 [4, 32768, 153], P('dp', 'graph'), may hold values from -0.119628906 to 0.119628906
Outputs:
- logits: float32 [4, 32768, 153], P('dp', 'graph')
- g_w1_self: float32 [768, 1024], P('feat')
- g_w1_neigh: float32 [768, 1024], P('feat')
- g_w2_self: float32 [1024, 153], P('feat')
- g_w2_neigh: float32 [1024, 153], P('feat')
The draws below stay inside these ranges and needn't reach their ends.
Inputs may be any that keep to these rules, and one draw needn't show every extreme that they name: `tile_rows`: row blocks 3 * 4 and above of every partition hold frontier nodes and are named by no slot. `tile_cols`: the column blocks of the 3 slots of one partition and one owner are distinct, dead slots included. `tile_count`: in every minibatch some owner has 3 live slots in every partition.
All inputs are finite; a program needn't handle non-finite values. No bound on the sum of `tile_bits` on one device may be relied on, other than what follows from the above.
Results may differ from the reference program's by a relative error of at most 0.0045.
Values may be sent and summed in bfloat16 or wider, within the bound.
A program may use at most 128 MiB of HBM per device.

```python
import jax
import jax.numpy as jnp
from jax import lax

F = 768
H = 1024
C = 153
TILE = 128
TPO = 3
BLK_DEV = 16
NODE_DEV = 2048
NODES = 32768
N_GRAPH = 16
N_DP = 4


def draw_tile_rows(key, part):
    key = jax.random.fold_in(key, 5)
    return jax.random.randint(key, (N_DP, N_GRAPH, N_GRAPH, TPO), 0, 3 * BLK_DEV // 4).astype(jnp.int32)


def draw_tile_cols(key, part):
    key = jax.random.fold_in(key, 7)
    scores = jax.random.randint(key, (N_DP, N_GRAPH, N_GRAPH, BLK_DEV), 0, 2 ** 20) * BLK_DEV
    scores = scores + jnp.arange(BLK_DEV, dtype=jnp.int32)
    order = jnp.argsort(scores, axis=-1)
    return order[..., :TPO].astype(jnp.int32)


def draw_tile_count(key, part):
    key = jax.random.fold_in(key, 11)
    first, second = jax.random.split(key)
    counts = jax.random.randint(first, (N_DP, N_GRAPH, N_GRAPH), 0, TPO + 1)
    busiest = jax.random.randint(second, (N_DP,), 0, N_GRAPH)
    owners = jnp.arange(N_GRAPH, dtype=jnp.int32)
    return jnp.where(owners[None, None, :] == busiest[:, None, None], TPO, counts).astype(jnp.int32)


def place_ends(result, own_key, least, largest):
    place = [jax.random.randint(jax.random.fold_in(own_key, axis), (), 0, length) for axis, length in enumerate(result.shape)]
    longest = result.shape.index(max(result.shape))
    neighbour = place[:longest] + [(place[longest] + 1) % result.shape[longest]] + place[longest + 1:]
    return result.at[tuple(place)].set(least).at[tuple(neighbour)].set(largest)


def steps_of(key, extent, pieces, least, high):
    def one(position, blocks):
        draws = jax.random.uniform(jax.random.fold_in(jax.random.fold_in(key, 6), position), (blocks,), jnp.float32, least / len(pieces), high / len(pieces))
        return jnp.repeat(jnp.exp(draws), extent[position] // blocks).reshape((-1,) + (1,) * (len(extent) - position - 1))

    gain = one(*pieces[0])
    for cut in pieces[1:]:
        gain = gain * one(*cut)
    return gain


def centred(stream_key, shape, scale, limit, cuts=(), held_as=jnp.bfloat16):
    loudness = steps_of(stream_key, shape, cuts, -0.22, 0.18) if cuts else 1.0
    drawn = jax.random.normal(stream_key, shape, jnp.float32) * scale * loudness
    return jnp.minimum(jnp.maximum(drawn, -limit), limit).astype(held_as)


def setup_inputs(seed: int = 0) -> dict:
    splits = jax.random.split(jax.random.key(seed), 11)
    features = centred(splits[0], (N_DP, NODES, F), 1.0, 6.0, ((0, 4), (1, 16), (2, 4)))
    w1_self = centred(splits[1], (F, H), F ** -0.5, 0.21875, ((0, 4),))
    w1_neigh = centred(splits[2], (F, H), (F // 9) ** -0.5, 0.625, ((0, 4),))
    w2_self = centred(splits[3], (H, C), H ** -0.5, 0.1875, ((0, 4),))
    w2_neigh = centred(splits[4], (H, C), (H // 9) ** -0.5, 0.5, ((0, 4),))
    tile_rows = draw_tile_rows(jax.random.fold_in(splits[10], 71), 0)
    tile_cols = draw_tile_cols(jax.random.fold_in(splits[10], 71), 0)
    tile_count = draw_tile_count(jax.random.fold_in(splits[10], 71), 0)
    tile_bits = place_ends((jax.random.randint(splits[8], (N_DP, N_GRAPH, N_GRAPH, TPO, TILE, TILE), 0, 8) < 1).astype(jnp.int32), jax.random.fold_in(splits[8], 1), 0, 1)
    d_logits = centred(splits[9], (N_DP, NODES, C), 0.02, 0.119628906, ((0, 4), (1, 16)))
    return dict(features=features, w1_self=w1_self, w1_neigh=w1_neigh, w2_self=w2_self, w2_neigh=w2_neigh, tile_rows=tile_rows, tile_cols=tile_cols, tile_count=tile_count, tile_bits=tile_bits, d_logits=d_logits)


highest = lax.Precision.HIGHEST


def degrees(slot_rows, slot_bits, is_live):
    block_ids = jnp.arange(BLK_DEV, dtype=jnp.int32)
    totals = jnp.sum(slot_bits, axis=4)
    onehot = ((slot_rows[None] == block_ids[:, None, None, None]) & is_live[None]).astype(jnp.float32)
    counts = jnp.einsum("rgos,gosi->gri", onehot, totals, precision=highest)
    return counts.reshape(NODES)


def aggregate(source, slot_rows, slot_cols, slot_bits, is_live):
    width = source.shape[1]
    blocks = source.reshape(N_GRAPH, BLK_DEV, TILE, width)
    owners = jnp.arange(N_GRAPH, dtype=jnp.int32)[:, None]
    block_ids = jnp.arange(BLK_DEV, dtype=jnp.int32)

    def partition(group):
        fetched = blocks[owners, slot_cols[group]].astype(jnp.float32)
        terms = jnp.einsum("osij,osjw->osiw", slot_bits[group], fetched, precision=highest)
        onehot = ((slot_rows[group][None] == block_ids[:, None, None]) & is_live[group][None]).astype(jnp.float32)
        summed = jnp.einsum("ros,osiw->riw", onehot, terms, precision=highest)
        return summed.reshape(NODE_DEV, width)

    return lax.map(partition, jnp.arange(N_GRAPH, dtype=jnp.int32)).reshape(NODES, width)


def transpose_aggregate(source, slot_rows, slot_cols, slot_bits):
    width = source.shape[1]
    blocks = source.reshape(N_GRAPH, BLK_DEV, TILE, width)
    block_ids = jnp.arange(BLK_DEV, dtype=jnp.int32)

    def partition(group):
        picked = blocks[group][slot_rows[group]].astype(jnp.float32)
        terms = jnp.einsum("osij,osiw->osjw", slot_bits[group], picked, precision=highest)
        return terms.astype(jnp.bfloat16)

    all_terms = lax.map(partition, jnp.arange(N_GRAPH, dtype=jnp.int32))

    def owner(target):
        onehot = (slot_cols[:, target][None] == block_ids[:, None, None]).astype(jnp.float32)
        owner_terms = all_terms[:, target].astype(jnp.float32)
        summed = jnp.einsum("cgs,gsjw->cjw", onehot, owner_terms, precision=highest)
        return summed.reshape(NODE_DEV, width)

    return lax.map(owner, jnp.arange(N_GRAPH, dtype=jnp.int32)).reshape(NODES, width)


def reference(features, w1_self, w1_neigh, w2_self, w2_neigh, tile_rows, tile_cols, tile_count, tile_bits, d_logits):
    slot_ids = jnp.arange(TPO, dtype=jnp.int32)

    def minibatch(batch):
        slot_rows = tile_rows[batch]
        slot_cols = tile_cols[batch]
        is_live = slot_ids < tile_count[batch][..., None]
        slot_bits = jnp.where(is_live[..., None, None], tile_bits[batch], 0).astype(jnp.float32)
        inverse = (1.0 / jnp.maximum(degrees(slot_rows, slot_bits, is_live), 1.0))[:, None]
        own_feats = features[batch]
        neigh_feats = (inverse * aggregate(own_feats, slot_rows, slot_cols, slot_bits, is_live)).astype(jnp.bfloat16)
        pre_act = jnp.dot(own_feats, w1_self, preferred_element_type=jnp.float32) + jnp.dot(neigh_feats, w1_neigh, preferred_element_type=jnp.float32)
        hidden = jax.nn.silu(pre_act).astype(jnp.bfloat16)
        neigh_mean = (inverse * aggregate(hidden, slot_rows, slot_cols, slot_bits, is_live)).astype(jnp.bfloat16)
        logits = jnp.dot(hidden, w2_self, preferred_element_type=jnp.float32) + jnp.dot(neigh_mean, w2_neigh, preferred_element_type=jnp.float32)
        grad_out = d_logits[batch]
        grad_second_self = jnp.dot(hidden.T, grad_out, preferred_element_type=jnp.float32)
        grad_second_neigh = jnp.dot(neigh_mean.T, grad_out, preferred_element_type=jnp.float32)
        scaled_two = (inverse * jnp.dot(grad_out, w2_neigh.T, preferred_element_type=jnp.float32)).astype(jnp.bfloat16)
        grad_hidden = jnp.dot(grad_out, w2_self.T, preferred_element_type=jnp.float32) + transpose_aggregate(scaled_two, slot_rows, slot_cols, slot_bits)
        logistic = jax.nn.sigmoid(pre_act)
        grad_pre_low = (grad_hidden * logistic * (1.0 + pre_act * (1.0 - logistic))).astype(jnp.bfloat16)
        grad_first_self = jnp.dot(own_feats.T, grad_pre_low, preferred_element_type=jnp.float32)
        grad_first_neigh = jnp.dot(neigh_feats.T, grad_pre_low, preferred_element_type=jnp.float32)
        return logits, (grad_first_self, grad_first_neigh, grad_second_self, grad_second_neigh)

    logits, grads = lax.map(minibatch, jnp.arange(N_DP, dtype=jnp.int32))
    return logits, jnp.sum(grads[0], axis=0), jnp.sum(grads[1], axis=0), jnp.sum(grads[2], axis=0), jnp.sum(grads[3], axis=0)
```

```python
import functools

import jax
import jax.numpy as jnp
from jax import lax
from jax.experimental import pallas as pl
from jax.experimental.pallas import tpu as pltpu
from jax.sharding import PartitionSpec as P

MESH = pl.DeviceIdType.MESH
TILE = 128
CPAD = 192
BF16, F32, I32 = jnp.bfloat16, jnp.float32, jnp.int32
NT = (((1,), (1,)), ((), ()))


def dot(a, b):
    return jnp.dot(a, b, preferred_element_type=F32)


def dot_nt(a, b):
    return lax.dot_general(a, b, NT, preferred_element_type=F32)


def loop(lo, hi, body):
    def step(i, carry):
        body(i)
        return carry

    lax.fori_loop(lo, hi, step, 0)


def spread_order(k, n):
    return n // 2 + ((k + 0) // 2) * (1 - 2 * (k % 2))


def lanes(start, size):
    return pl.ds(pl.multiple_of(start, TILE), size)


class RingGather:
    def __init__(self, buf, rows, cols, ssem, rsem, x, nx):
        self.buf, self.rows, self.cols, self.ssem, self.rsem, self.x, self.nx = buf, rows, cols, ssem, rsem, x, nx

    def copy(self, owner, first, count, which, to):
        part = self.buf.at[pl.ds(pl.multiple_of(owner * self.rows, 16), self.rows), pl.ds(first, count)]
        return pltpu.make_async_remote_copy(
            src_ref=part,
            dst_ref=part,
            send_sem=self.ssem.at[which],
            recv_sem=self.rsem.at[which],
            device_id={"feat": to},
            device_id_type=MESH,
        )

    def parts(self):
        x, nx, c = self.x, self.nx, self.cols
        right, left = lax.rem(x + 1, nx), lax.rem(x + nx - 1, nx)
        return (
            self.copy(x, 0, c, 0, right),
            self.copy(x, 0, c, 1, left),
            self.copy(left, 0, c // 2, 2, right),
            self.copy(right, c // 2, c // 2, 3, left),
        )

    def start(self):
        a, b, _, _ = self.parts()
        a.start()
        b.start()

    def middle(self):
        a, b, c, d = self.parts()
        a.wait_recv()
        c.start()
        b.wait_recv()
        d.start()

    def finish(self):
        a, b, c, d = self.parts()
        c.wait_recv()
        d.wait_recv()
        for p in (a, b, c, d):
            p.wait_send()


def exchange_kernel(
    n_graph,
    n_feat,
    rows_s,
    count_s,
    cols_v,
    feat_v,
    dl_v,
    bits_v,
    w1s_v,
    w1n_v,
    feat_o,
    ax_o,
    q_o,
    inv_o,
    req_o,
    w1s_o,
    w1n_o,
    featb,
    send,
    arr,
    adj,
    live,
    acc,
    dinv,
    qsend,
    qarr,
    req_s,
    sem_local,
    sem_req_s,
    sem_req_r,
    sem_f_s,
    sem_f_r,
    sem_q_s,
    sem_q_r,
    sem_w_s,
    sem_w_r,
    sem_g_s,
    sem_g_r,
):
    g = lax.axis_index("graph")
    x = lax.axis_index("feat")
    width, nodes = featb.shape[1], feat_o.shape[1]
    n_rows = adj.shape[0]
    row_blocks = n_rows // TILE
    blocks = nodes // TILE
    tpo = 3
    pair = tpo * TILE

    barrier = pltpu.get_barrier_semaphore()

    def greet(d):
        pl.semaphore_signal(barrier, inc=1, device_id={"graph": lax.rem(g + d, n_graph)}, device_id_type=MESH)

    loop(1, n_graph, greet)
    for d in range(1, n_feat):
        pl.semaphore_signal(barrier, inc=1, device_id={"feat": lax.rem(x + d, n_feat)}, device_id_type=MESH)

    iota_r = lax.broadcasted_iota(I32, (width, width), 0)
    iota_c = lax.broadcasted_iota(I32, (width, width), 1)
    eye = (iota_r == iota_c).astype(F32).astype(BF16)
    own_rows = pl.ds(pl.multiple_of(x * width, 16), width)

    def turn(b):
        t = dot_nt(eye, feat_v[pl.ds(pl.multiple_of(b * TILE, TILE), TILE), :]).astype(BF16)
        featb[b] = t
        feat_o[own_rows, lanes(b * TILE, TILE)] = t

    loop(0, blocks, turn)
    req_o[g] = cols_v[g]

    pl.semaphore_wait(barrier, n_graph - 1 + n_feat - 1)

    def request(d):
        to = lax.rem(g + d, n_graph)
        return pltpu.make_async_remote_copy(
            src_ref=cols_v.at[to],
            dst_ref=req_o.at[g],
            send_sem=sem_req_s.at[d],
            recv_sem=sem_req_r.at[d],
            device_id={"graph": to},
            device_id_type=MESH,
        )

    loop(1, n_graph, lambda d: request(d).start())

    gather_feat = RingGather(feat_o, width, nodes, sem_g_s.at[0], sem_g_r.at[0], x, n_feat)
    gather_ax = RingGather(ax_o, width, n_rows, sem_g_s.at[1], sem_g_r.at[1], x, n_feat)
    gather_q = RingGather(q_o, CPAD // n_feat, nodes, sem_g_s.at[2], sem_g_r.at[2], x, n_feat)
    gather_feat.start()

    hidden = w1s_o.shape[1]

    def weights(d, k):
        to = lax.rem(x + d, n_feat)
        src, dst = ((w1s_v, w1s_o), (w1n_v, w1n_o))[k]
        return pltpu.make_async_remote_copy(
            src_ref=src.at[:, lanes(to * hidden, hidden)],
            dst_ref=dst.at[own_rows, :],
            send_sem=sem_w_s.at[k, d],
            recv_sem=sem_w_r.at[k, d],
            device_id={"feat": to},
            device_id_type=MESH,
        )

    deg_ones = jnp.ones((8, TILE), BF16)
    acc_deg = inv_o

    acc_deg[...] = jnp.zeros(acc_deg.shape, F32)

    def prepare(o):
        for s in range(tpo):
            t = o * tpo + s
            on = (s < count_s[o]).astype(I32)
            tile = (bits_v[t] * on).astype(F32)
            live[t] = tile.astype(BF16)

    loop(0, n_graph, prepare)

    def take(d):
        request(d).wait_recv()

    loop(1, n_graph, take)
    fetch = pltpu.make_async_copy(req_o, req_s, sem_local)
    fetch.start()
    fetch.wait()

    def feats(d):
        to = lax.rem(g + d, n_graph)
        return pltpu.make_async_remote_copy(
            src_ref=send.at[to],
            dst_ref=arr.at[g],
            send_sem=sem_f_s.at[d],
            recv_sem=sem_f_r.at[d],
            device_id={"graph": to},
            device_id_type=MESH,
        )

    def post(k):
        d = spread_order(k, n_graph)
        to = lax.rem(g + d, n_graph)
        for s in range(tpo):
            send[to, :, s * TILE : (s + 1) * TILE] = featb[req_s[to, 0, s]]
        feats(d).start()

    loop(1, n_graph, post)
    for s in range(tpo):
        arr[g, :, s * TILE : (s + 1) * TILE] = featb[req_s[g, 0, s]]

    for k in range(2):
        for d in range(1, n_feat):
            weights(d, k).start()
        src, dst = ((w1s_v, w1s_o), (w1n_v, w1n_o))[k]
        dst[own_rows, :] = src[:, lanes(x * hidden, hidden)]

    def build(o):
        for s in range(tpo):
            t = o * tpo + s
            tile = live[t].astype(F32)
            row = rows_s[o, s]
            for r in range(row_blocks):
                here = (row == r).astype(F32)
                adj[r * TILE : (r + 1) * TILE, lanes(t * TILE, TILE)] = (tile * here).astype(BF16)

    loop(0, n_graph, build)

    def degree(o):
        acc_deg[:, :n_rows] += dot_nt(jnp.ones((8, pair), BF16), adj[:, lanes(o * pair, pair)])

    loop(0, n_graph, degree)
    inv_o[...] = 1.0 / jnp.maximum(acc_deg[...], 1.0)

    share = CPAD // n_feat
    own_classes = pl.ds(pl.multiple_of(x * share, 16), share)
    for r in range(row_blocks):
        here = slice(r * TILE, (r + 1) * TILE)
        dinv[r] = (dl_v[own_classes, here].astype(F32) * inv_o[0:1, here]).astype(BF16)

    def q_terms(d):
        to = lax.rem(g + d, n_graph)
        return pltpu.make_async_remote_copy(
            src_ref=qsend.at[to],
            dst_ref=qarr.at[g, pl.ds(0, tpo)],
            send_sem=sem_q_s.at[d],
            recv_sem=sem_q_r.at[d],
            device_id={"graph": to},
            device_id_type=MESH,
        )

    def terms(k):
        d = spread_order(k, n_graph)
        to = lax.rem(g + d, n_graph)
        for s in range(tpo):
            qsend[to, s] = dot(dinv[rows_s[to, s]], live[to * tpo + s]).astype(BF16)
        q_terms(d).start()

    loop(1, n_graph, terms)
    for s in range(tpo):
        qarr[g, s] = dot(dinv[rows_s[g, s]], live[g * tpo + s]).astype(BF16)

    def blank(o):
        qarr[o, tpo] = jnp.zeros((share, TILE), BF16)

    loop(0, n_graph, blank)

    gather_feat.middle()

    def add(o):
        acc[...] += dot_nt(arr[o], adj[:, lanes(o * pair, pair)])

    acc[...] = jnp.zeros(acc.shape, F32)
    add(g)

    def arrive(k):
        d = spread_order(n_graph - k, n_graph)
        feats(d).wait_recv()
        add(lax.rem(g + n_graph - d, n_graph))

    loop(1, n_graph, arrive)
    ax_o[own_rows, :] = (acc[...] * inv_o[0:1, :n_rows]).astype(BF16)
    gather_ax.start()

    loop(1, n_graph, lambda d: q_terms(d).wait_recv())

    def column(c):
        def source(o, total):
            which = jnp.where(
                req_s[o, 0, 0] == c, 0, jnp.where(req_s[o, 0, 1] == c, 1, jnp.where(req_s[o, 0, 2] == c, 2, tpo))
            )
            return total + qarr[o, which].astype(F32)

        total = lax.fori_loop(0, n_graph, source, jnp.zeros((share, TILE), F32))
        q_o[own_classes, lanes(c * TILE, TILE)] = total.astype(BF16)

    loop(0, blocks, column)
    gather_q.start()
    gather_ax.middle()
    gather_q.middle()

    def settle(d):
        request(d).wait_send()
        feats(d).wait_send()
        q_terms(d).wait_send()

    loop(1, n_graph, settle)
    for k in range(2):
        for d in range(1, n_feat):
            weights(d, k).wait()
    gather_feat.finish()
    gather_ax.finish()
    gather_q.finish()


def exchange(n_graph, n_feat, rows, counts, cols, feats, dl_t, bits, w1s, w1n):
    nodes, width = feats.shape
    n_slots, tpo = bits.shape[0], rows.shape[1]
    n_rows = nodes // 4 * 3
    share = CPAD // n_feat
    hidden = w1s.shape[1] // n_feat
    vmem = pl.BlockSpec(memory_space=pltpu.VMEM)
    smem = pl.BlockSpec(memory_space=pltpu.SMEM)
    dma = pltpu.SemaphoreType.DMA
    blocks = nodes // TILE
    cols_wide = jnp.zeros((n_graph, 1, TILE), I32).at[:, 0, :tpo].set(cols)
    return pl.pallas_call(
        functools.partial(exchange_kernel, n_graph, n_feat),
        out_shape=(
            jax.ShapeDtypeStruct((n_feat * width, nodes), BF16),
            jax.ShapeDtypeStruct((n_feat * width, n_rows), BF16),
            jax.ShapeDtypeStruct((CPAD, nodes), BF16),
            jax.ShapeDtypeStruct((8, nodes), F32),
            jax.ShapeDtypeStruct((n_graph, 1, TILE), I32),
            jax.ShapeDtypeStruct((n_feat * width, hidden), BF16),
            jax.ShapeDtypeStruct((n_feat * width, hidden), BF16),
        ),
        in_specs=[smem, smem, vmem, vmem, vmem, vmem, vmem, vmem],
        out_specs=(vmem,) * 7,
        scratch_shapes=[
            pltpu.VMEM((blocks, width, TILE), BF16),
            pltpu.VMEM((n_graph, width, tpo * TILE), BF16),
            pltpu.VMEM((n_graph, width, tpo * TILE), BF16),
            pltpu.VMEM((n_rows, n_slots * TILE), BF16),
            pltpu.VMEM((n_slots, TILE, TILE), BF16),
            pltpu.VMEM((width, n_rows), F32),
            pltpu.VMEM((n_rows // TILE, share, TILE), BF16),
            pltpu.VMEM((n_graph, tpo, share, TILE), BF16),
            pltpu.VMEM((n_graph, tpo + 1, share, TILE), BF16),
            pltpu.SMEM((n_graph, 1, TILE), I32),
            dma,
            dma((n_graph,)),
            dma((n_graph,)),
            dma((n_graph,)),
            dma((n_graph,)),
            dma((n_graph,)),
            dma((n_graph,)),
            dma((2, n_feat)),
            dma((2, n_feat)),
            dma((3, 4)),
            dma((3, 4)),
        ],
        compiler_params=pltpu.CompilerParams(
            collective_id=0, has_side_effects=True, vmem_limit_bytes=56 * 1024 * 1024
        ),
    )(rows, counts, cols_wide, feats, dl_t, bits, w1s, w1n)


def on_device(
    n_graph,
    n_feat,
    features,
    w1_self,
    w1_neigh,
    w2_self,
    w2_neigh,
    tile_rows,
    tile_cols,
    tile_count,
    tile_bits,
    d_logits,
):
    feats = features[0]
    rows, cols, counts = tile_rows[0, 0], tile_cols[0, 0], tile_count[0, 0]
    bits = tile_bits[0, 0].reshape(-1, TILE, TILE)
    nodes = feats.shape[0]
    n_slots, tpo = bits.shape[0], rows.shape[1]
    blocks = nodes // TILE
    n_rows = nodes // 4 * 3
    classes = d_logits.shape[2]
    share = CPAD // n_feat
    dl_t = jnp.pad(d_logits[0].T, ((0, CPAD - classes), (0, 0)))

    feat_t, ax_t, q_t, inv, requested, w1s, w1n = exchange(
        n_graph, n_feat, rows, counts, cols, feats, dl_t, bits, w1_self, w1_neigh
    )
    inv = inv[0]

    w2s = jnp.pad(w2_self, ((0, 0), (0, CPAD - classes)))
    w2n = jnp.pad(w2_neigh, ((0, 0), (0, CPAD - classes)))

    pre = jnp.einsum("fh,fn->hn", w1s, feat_t, preferred_element_type=F32)
    pre = pre + jnp.pad(
        jnp.einsum("fh,fn->hn", w1n, ax_t, preferred_element_type=F32), ((0, 0), (0, nodes - n_rows))
    )
    logistic = jax.nn.sigmoid(pre)
    hidden = (pre * logistic).astype(BF16)
    p_self = jnp.einsum("hc,hn->cn", w2s, hidden, preferred_element_type=F32)
    p_neigh = jnp.einsum("hc,hn->cn", w2n, hidden, preferred_element_type=F32)

    p_neigh = lax.psum_scatter(p_neigh.astype(BF16), "feat", scatter_dimension=0, tiled=True)
    blocked = p_neigh.astype(BF16).reshape(share, blocks, TILE).transpose(1, 0, 2)
    picked = blocked[requested[:, 0, :tpo]]
    arrived = lax.all_to_all(picked, "graph", split_axis=0, concat_axis=0, tiled=True)
    is_live = jnp.arange(tpo, dtype=I32)[None, :] < counts[:, None]
    live_bits = jnp.where(is_live[:, :, None, None], tile_bits[0, 0], 0).astype(BF16)
    terms = jnp.einsum("osij,oscj->osci", live_bits, arrived, preferred_element_type=F32)
    onehot = ((rows[None] == jnp.arange(blocks, dtype=I32)[:, None, None]) & is_live[None]).astype(F32)
    summed = jnp.einsum("ros,osci->cri", onehot, terms, precision=lax.Precision.HIGHEST).reshape(share, nodes)
    p_self = lax.psum_scatter(p_self, "feat", scatter_dimension=0, tiled=True)
    logits_t = lax.all_gather(p_self + inv[None] * summed, "feat", axis=0, tiled=True)
    logits = logits_t[:classes].T

    d_hidden = jnp.einsum("hc,cn->hn", w2s, dl_t, preferred_element_type=F32) + jnp.einsum(
        "hc,cn->hn", w2n, q_t, preferred_element_type=F32
    )
    d_pre = (d_hidden * logistic * (1.0 + pre * (1.0 - logistic))).astype(BF16)
    g1s = jnp.einsum("fn,hn->fh", feat_t, d_pre, preferred_element_type=F32)
    g1n = jnp.einsum("fn,hn->fh", ax_t, d_pre[:, :n_rows], preferred_element_type=F32)
    g2s = jnp.einsum("hn,cn->hc", hidden, dl_t, preferred_element_type=F32)
    g2n = jnp.einsum("hn,cn->hc", hidden, q_t, preferred_element_type=F32)
    g1s = lax.all_to_all(g1s, "feat", split_axis=0, concat_axis=1, tiled=True)
    g1n = lax.all_to_all(g1n, "feat", split_axis=0, concat_axis=1, tiled=True)
    g1s, g1n, g2s, g2n = lax.psum((g1s, g1n, g2s, g2n), ("graph", "dp"))
    return logits[None], g1s, g1n, g2s[:, :classes], g2n[:, :classes]


def solution(mesh):
    placed = (
        P("dp", "graph", "feat"),
        P("feat", None),
        P("feat", None),
        P("feat", None),
        P("feat", None),
        P("dp", "graph", None, None),
        P("dp", "graph", None, None),
        P("dp", "graph", None),
        P("dp", "graph", None, None, None, None),
        P("dp", "graph", None),
    )
    return jax.shard_map(
        functools.partial(on_device, mesh.shape["graph"], mesh.shape["feat"]),
        mesh=mesh,
        in_specs=placed,
        out_specs=(
            P("dp", "graph", None),
            P("feat", None),
            P("feat", None),
            P("feat", None),
            P("feat", None),
        ),
        check_vma=False,
    )
```

```python
import functools

import jax
import jax.numpy as jnp
from jax import lax
from jax.experimental import pallas as pl
from jax.experimental.pallas import tpu as pltpu
from jax.sharding import PartitionSpec as P

MESH = pl.DeviceIdType.MESH
TILE = 128
CPAD = 192
BF16, F32, I32 = jnp.bfloat16, jnp.float32, jnp.int32
NT = (((1,), (1,)), ((), ()))


def dot(a, b):
    return jnp.dot(a, b, preferred_element_type=F32)


def dot_nt(a, b):
    return lax.dot_general(a, b, NT, preferred_element_type=F32)


def loop(lo, hi, body):
    def step(i, carry):
        body(i)
        return carry

    lax.fori_loop(lo, hi, step, 0)


def spread_order(k, n):
    return n // 2 + ((k + 0) // 2) * (1 - 2 * (k % 2))


def lanes(start, size):
    return pl.ds(pl.multiple_of(start, TILE), size)


class RingGather:
    def __init__(self, buf, rows, cols, ssem, rsem, x, nx):
        self.buf, self.rows, self.cols, self.ssem, self.rsem, self.x, self.nx = buf, rows, cols, ssem, rsem, x, nx

    def copy(self, owner, first, count, which, to):
        part = self.buf.at[pl.ds(pl.multiple_of(owner * self.rows, 16), self.rows), pl.ds(first, count)]
        return pltpu.make_async_remote_copy(
            src_ref=part,
            dst_ref=part,
            send_sem=self.ssem.at[which],
            recv_sem=self.rsem.at[which],
            device_id={"feat": to},
            device_id_type=MESH,
        )

    def parts(self):
        x, nx, c = self.x, self.nx, self.cols
        right, left = lax.rem(x + 1, nx), lax.rem(x + nx - 1, nx)
        return (
            self.copy(x, 0, c, 0, right),
            self.copy(x, 0, c, 1, left),
            self.copy(left, 0, c // 2, 2, right),
            self.copy(right, c // 2, c // 2, 3, left),
        )

    def start(self):
        a, b, _, _ = self.parts()
        a.start()
        b.start()

    def middle(self):
        a, b, c, d = self.parts()
        a.wait_recv()
        c.start()
        b.wait_recv()
        d.start()

    def finish(self):
        a, b, c, d = self.parts()
        c.wait_recv()
        d.wait_recv()
        for p in (a, b, c, d):
            p.wait_send()


def identity(size):
    return (lax.broadcasted_iota(I32, (size, size), 0) == lax.broadcasted_iota(I32, (size, size), 1)).astype(F32).astype(BF16)


def exchange_kernel(
    n_graph,
    n_feat,
    rows_s,
    count_s,
    cols_v,
    feat_v,
    dl_v,
    bits_v,
    w1s_v,
    w1n_v,
    feat_o,
    ax_o,
    q_o,
    inv_o,
    req_o,
    w1s_o,
    w1n_o,
    featb,
    send,
    arr,
    adj,
    live,
    acc,
    dinv,
    qsend,
    qarr,
    req_s,
    sem_local,
    sem_req_s,
    sem_req_r,
    sem_f_s,
    sem_f_r,
    sem_q_s,
    sem_q_r,
    sem_w_s,
    sem_w_r,
    sem_g_s,
    sem_g_r,
):
    g = lax.axis_index("graph")
    x = lax.axis_index("feat")
    width, nodes = featb.shape[1], feat_o.shape[1]
    n_rows = adj.shape[0]
    row_blocks = n_rows // TILE
    blocks = nodes // TILE
    tpo = 3
    pair = tpo * TILE

    barrier = pltpu.get_barrier_semaphore()

    def greet(d):
        pl.semaphore_signal(barrier, inc=1, device_id={"graph": lax.rem(g + d, n_graph)}, device_id_type=MESH)

    loop(1, n_graph, greet)
    for d in range(1, n_feat):
        pl.semaphore_signal(barrier, inc=1, device_id={"feat": lax.rem(x + d, n_feat)}, device_id_type=MESH)

    eye = identity(width)
    own_rows = pl.ds(pl.multiple_of(x * width, 16), width)

    def turn(b):
        t = dot_nt(eye, feat_v[pl.ds(pl.multiple_of(b * TILE, TILE), TILE), :]).astype(BF16)
        featb[b] = t
        feat_o[own_rows, lanes(b * TILE, TILE)] = t

    loop(0, blocks, turn)
    req_o[g] = cols_v[g]

    pl.semaphore_wait(barrier, n_graph - 1 + n_feat - 1)

    def request(d):
        to = lax.rem(g + d, n_graph)
        return pltpu.make_async_remote_copy(
            src_ref=cols_v.at[to],
            dst_ref=req_o.at[g],
            send_sem=sem_req_s.at[d],
            recv_sem=sem_req_r.at[d],
            device_id={"graph": to},
            device_id_type=MESH,
        )

    loop(1, n_graph, lambda d: request(d).start())

    gather_feat = RingGather(feat_o, width, nodes, sem_g_s.at[0], sem_g_r.at[0], x, n_feat)
    gather_ax = RingGather(ax_o, width, n_rows, sem_g_s.at[1], sem_g_r.at[1], x, n_feat)
    gather_q = RingGather(q_o, CPAD // n_feat, nodes, sem_g_s.at[2], sem_g_r.at[2], x, n_feat)
    gather_feat.start()

    hidden = w1s_o.shape[1]

    def weights(d, k):
        to = lax.rem(x + d, n_feat)
        src, dst = ((w1s_v, w1s_o), (w1n_v, w1n_o))[k]
        return pltpu.make_async_remote_copy(
            src_ref=src.at[:, lanes(to * hidden, hidden)],
            dst_ref=dst.at[own_rows, :],
            send_sem=sem_w_s.at[k, d],
            recv_sem=sem_w_r.at[k, d],
            device_id={"feat": to},
            device_id_type=MESH,
        )

    deg_ones = jnp.ones((8, TILE), BF16)
    acc_deg = inv_o

    acc_deg[...] = jnp.zeros(acc_deg.shape, F32)

    def prepare(o):
        for s in range(tpo):
            t = o * tpo + s
            on = (s < count_s[o]).astype(I32)
            tile = (bits_v[t] * on).astype(F32)
            live[t] = tile.astype(BF16)

    loop(0, n_graph, prepare)

    def take(d):
        request(d).wait_recv()

    loop(1, n_graph, take)
    fetch = pltpu.make_async_copy(req_o, req_s, sem_local)
    fetch.start()
    fetch.wait()

    def feats(d):
        to = lax.rem(g + d, n_graph)
        return pltpu.make_async_remote_copy(
            src_ref=send.at[to],
            dst_ref=arr.at[g],
            send_sem=sem_f_s.at[d],
            recv_sem=sem_f_r.at[d],
            device_id={"graph": to},
            device_id_type=MESH,
        )

    def post(k):
        d = spread_order(k, n_graph)
        to = lax.rem(g + d, n_graph)
        for s in range(tpo):
            send[to, :, s * TILE : (s + 1) * TILE] = featb[req_s[to, 0, s]]
        feats(d).start()

    loop(1, n_graph, post)
    for s in range(tpo):
        arr[g, :, s * TILE : (s + 1) * TILE] = featb[req_s[g, 0, s]]

    for k in range(2):
        for d in range(1, n_feat):
            weights(d, k).start()
        src, dst = ((w1s_v, w1s_o), (w1n_v, w1n_o))[k]
        dst[own_rows, :] = src[:, lanes(x * hidden, hidden)]

    def build(o):
        for s in range(tpo):
            t = o * tpo + s
            tile = live[t].astype(F32)
            row = rows_s[o, s]
            for r in range(row_blocks):
                here = (row == r).astype(F32)
                adj[r * TILE : (r + 1) * TILE, lanes(t * TILE, TILE)] = (tile * here).astype(BF16)

    loop(0, n_graph, build)

    def degree(o):
        acc_deg[:, :n_rows] += dot_nt(jnp.ones((8, pair), BF16), adj[:, lanes(o * pair, pair)])

    loop(0, n_graph, degree)
    inv_o[...] = 1.0 / jnp.maximum(acc_deg[...], 1.0)

    share = CPAD // n_feat
    own_classes = pl.ds(pl.multiple_of(x * share, 16), share)
    for r in range(row_blocks):
        here = slice(r * TILE, (r + 1) * TILE)
        dinv[r] = (dl_v[own_classes, here].astype(F32) * inv_o[0:1, here]).astype(BF16)

    def q_terms(d):
        to = lax.rem(g + d, n_graph)
        return pltpu.make_async_remote_copy(
            src_ref=qsend.at[to],
            dst_ref=qarr.at[g, pl.ds(0, tpo)],
            send_sem=sem_q_s.at[d],
            recv_sem=sem_q_r.at[d],
            device_id={"graph": to},
            device_id_type=MESH,
        )

    def terms(k):
        d = spread_order(k, n_graph)
        to = lax.rem(g + d, n_graph)
        for s in range(tpo):
            qsend[to, s] = dot(dinv[rows_s[to, s]], live[to * tpo + s]).astype(BF16)
        q_terms(d).start()

    loop(1, n_graph, terms)
    for s in range(tpo):
        qarr[g, s] = dot(dinv[rows_s[g, s]], live[g * tpo + s]).astype(BF16)

    def blank(o):
        qarr[o, tpo] = jnp.zeros((share, TILE), BF16)

    loop(0, n_graph, blank)

    gather_feat.middle()

    def add(o):
        acc[...] += dot_nt(arr[o], adj[:, lanes(o * pair, pair)])

    acc[...] = jnp.zeros(acc.shape, F32)
    add(g)

    def arrive(k):
        d = spread_order(n_graph - k, n_graph)
        feats(d).wait_recv()
        add(lax.rem(g + n_graph - d, n_graph))

    loop(1, n_graph, arrive)
    ax_o[own_rows, :] = (acc[...] * inv_o[0:1, :n_rows]).astype(BF16)
    gather_ax.start()

    loop(1, n_graph, lambda d: q_terms(d).wait_recv())

    def column(c):
        def source(o, total):
            which = jnp.where(
                req_s[o, 0, 0] == c, 0, jnp.where(req_s[o, 0, 1] == c, 1, jnp.where(req_s[o, 0, 2] == c, 2, tpo))
            )
            return total + qarr[o, which].astype(F32)

        total = lax.fori_loop(0, n_graph, source, jnp.zeros((share, TILE), F32))
        q_o[own_classes, lanes(c * TILE, TILE)] = total.astype(BF16)

    loop(0, blocks, column)
    gather_q.start()
    gather_ax.middle()
    gather_q.middle()

    def settle(d):
        request(d).wait_send()
        feats(d).wait_send()
        q_terms(d).wait_send()

    loop(1, n_graph, settle)
    for k in range(2):
        for d in range(1, n_feat):
            weights(d, k).wait()
    gather_feat.finish()
    gather_ax.finish()
    gather_q.finish()


def exchange(n_graph, n_feat, rows, counts, cols, feats, dl_t, bits, w1s, w1n):
    nodes, width = feats.shape
    n_slots, tpo = bits.shape[0], rows.shape[1]
    n_rows = nodes // 4 * 3
    share = CPAD // n_feat
    hidden = w1s.shape[1] // n_feat
    vmem = pl.BlockSpec(memory_space=pltpu.VMEM)
    smem = pl.BlockSpec(memory_space=pltpu.SMEM)
    dma = pltpu.SemaphoreType.DMA
    blocks = nodes // TILE
    cols_wide = jnp.zeros((n_graph, 1, TILE), I32).at[:, 0, :tpo].set(cols)
    return pl.pallas_call(
        functools.partial(exchange_kernel, n_graph, n_feat),
        out_shape=(
            jax.ShapeDtypeStruct((n_feat * width, nodes), BF16),
            jax.ShapeDtypeStruct((n_feat * width, n_rows), BF16),
            jax.ShapeDtypeStruct((CPAD, nodes), BF16),
            jax.ShapeDtypeStruct((8, nodes), F32),
            jax.ShapeDtypeStruct((n_graph, 1, TILE), I32),
            jax.ShapeDtypeStruct((n_feat * width, hidden), BF16),
            jax.ShapeDtypeStruct((n_feat * width, hidden), BF16),
        ),
        in_specs=[smem, smem, vmem, vmem, vmem, vmem, vmem, vmem],
        out_specs=(vmem,) * 7,
        scratch_shapes=[
            pltpu.VMEM((blocks, width, TILE), BF16),
            pltpu.VMEM((n_graph, width, tpo * TILE), BF16),
            pltpu.VMEM((n_graph, width, tpo * TILE), BF16),
            pltpu.VMEM((n_rows, n_slots * TILE), BF16),
            pltpu.VMEM((n_slots, TILE, TILE), BF16),
            pltpu.VMEM((width, n_rows), F32),
            pltpu.VMEM((n_rows // TILE, share, TILE), BF16),
            pltpu.VMEM((n_graph, tpo, share, TILE), BF16),
            pltpu.VMEM((n_graph, tpo + 1, share, TILE), BF16),
            pltpu.SMEM((n_graph, 1, TILE), I32),
            dma,
            dma((n_graph,)),
            dma((n_graph,)),
            dma((n_graph,)),
            dma((n_graph,)),
            dma((n_graph,)),
            dma((n_graph,)),
            dma((2, n_feat)),
            dma((2, n_feat)),
            dma((3, 4)),
            dma((3, 4)),
        ],
        compiler_params=pltpu.CompilerParams(
            collective_id=0, has_side_effects=True, vmem_limit_bytes=56 * 1024 * 1024
        ),
    )(rows, counts, cols_wide, feats, dl_t, bits, w1s, w1n)


def update_kernel(
    n_graph,
    n_feat,
    n_dp,
    rows_s,
    count_s,
    req_s,
    feat_v,
    ax_v,
    q_v,
    dl_v,
    inv_v,
    w1s_v,
    w1n_v,
    w2s_v,
    w2n_v,
    bits_v,
    logits_o,
    g1s_o,
    g1n_o,
    g2s_o,
    g2n_o,
    w1st,
    w1nt,
    w2st,
    w2nt,
    hid,
    dpre,
    pn,
    ps,
    pnr,
    psr,
    pb,
    psend,
    parr,
    adj,
    live,
    acc,
    lt,
    grad,
    cs,
    cr,
    ys,
    yr,
    xs,
    tz,
    zr,
    fin,
    sem_p_s,
    sem_p_r,
    sem_a_s,
    sem_a_r,
    sem_l_s,
    sem_l_r,
    sem_c_s,
    sem_c_r,
    sem_y_s,
    sem_y_r,
    sem_x_s,
    sem_x_r,
    sem_z_s,
    sem_z_r,
    sem_zg_s,
    sem_zg_r,
    sem_yg_s,
    sem_yg_r,
    sem_cg_s,
    sem_cg_r,
):
    g = lax.axis_index("graph")
    x = lax.axis_index("feat")
    y = lax.axis_index("dp")
    core = lax.rem(g, 2)
    z = g // 2
    n_z = n_graph // 2
    sibling = g + 1 - 2 * core
    n_rows = adj.shape[0]
    row_blocks = n_rows // TILE
    nodes = feat_v.shape[1]
    blocks = nodes // TILE
    hidden = hid.shape[0]
    width = feat_v.shape[0] // n_feat
    share = CPAD // n_feat
    strip = width // n_dp
    tpo = 3
    pair = tpo * TILE
    classes = logits_o.shape[1]

    barrier = pltpu.get_barrier_semaphore()

    def greet(d):
        pl.semaphore_signal(barrier, inc=1, device_id={"graph": lax.rem(g + d, n_graph)}, device_id_type=MESH)

    loop(1, n_graph, greet)
    for d in range(1, n_feat):
        pl.semaphore_signal(barrier, inc=1, device_id={"feat": lax.rem(x + d, n_feat)}, device_id_type=MESH)
    for d in range(1, n_dp):
        pl.semaphore_signal(barrier, inc=1, device_id={"dp": lax.rem(y + d, n_dp)}, device_id_type=MESH)

    def send(src, dst, ssem, rsem, to):
        return pltpu.make_async_remote_copy(
            src_ref=src, dst_ref=dst, send_sem=ssem, recv_sem=rsem, device_id=to, device_id_type=MESH
        )

    eye = identity(hidden)
    w1st[...] = dot_nt(eye, w1s_v[...]).astype(BF16)
    w1nt[...] = dot_nt(eye, w1n_v[...]).astype(BF16)
    eye_c = identity(CPAD)
    w2st[...] = dot_nt(eye_c, w2s_v[...]).astype(BF16)
    w2nt[...] = dot_nt(eye_c, w2n_v[...]).astype(BF16)

    chunk = nodes // 4

    def layer(n, with_neighbours):
        here = lanes(n * chunk, chunk)
        pre = dot(w1st[...], feat_v[:, here])
        if with_neighbours:
            pre = pre + dot(w1nt[...], ax_v[:, here])
        sig = 1.0 / (1.0 + jnp.exp(-pre))
        act = (pre * sig).astype(BF16)
        hid[:, here] = act
        pn[:, here] = dot(w2nt[...], act).astype(BF16)
        ps[:, here] = dot(w2st[...], act).astype(BF16)
        back = dot(w2s_v[...], dl_v[:, here]) + dot(w2n_v[...], q_v[:, here])
        dpre[:, here] = (back * sig * (1.0 + pre * (1.0 - sig))).astype(BF16)

    loop(0, 3, lambda n: layer(n, True))
    layer(3, False)

    pl.semaphore_wait(barrier, n_graph - 1 + n_feat - 1 + n_dp - 1)

    def scatter(d, k):
        to = lax.rem(x + d, n_feat)
        src, dst = ((pn, pnr), (ps, psr))[k]
        return send(
            src.at[pl.ds(pl.multiple_of(to * share, 16), share), :],
            dst.at[x],
            sem_p_s.at[k, d],
            sem_p_r.at[k, d],
            {"feat": to},
        )

    for d in range(1, n_feat):
        scatter(d, 0).start()

    def gradients(k):
        src, cols, other = ((feat_v, nodes, dl_v), (ax_v, n_rows, q_v))[k]
        dp = dpre[:, :cols]

        def first(o):
            t = dot_nt(src[pl.ds(pl.multiple_of(o * width, 16), width), :], dp)
            for i in range(n_dp):
                grad[k, i, pl.ds(pl.multiple_of(o * strip, 16), strip), :] = t[i * strip : (i + 1) * strip]

        loop(0, n_feat, first)
        t = dot_nt(other[...], hid[...])
        for i in range(n_dp):
            grad[k, i, n_feat * strip :, :] = t[i * share : (i + 1) * share]

    gradients(0)
    gradients(1)
    cs[...] = grad[1 - core].astype(BF16)
    core_send = send(cs, cr, sem_c_s, sem_c_r, {"graph": sibling})
    core_send.start()
    for d in range(1, n_feat):
        scatter(d, 1).start()

    def prepare(o):
        for s in range(tpo):
            t = o * tpo + s
            on = (s < count_s[o]).astype(I32)
            tile = (bits_v[t] * on).astype(F32)
            row = rows_s[o, s]
            for r in range(row_blocks):
                here = (row == r).astype(F32)
                adj[r * TILE : (r + 1) * TILE, lanes(t * TILE, TILE)] = (tile * here).astype(BF16)

    loop(0, n_graph, prepare)

    for d in range(1, n_feat):
        scatter(d, 0).wait_recv()
    own_classes = pl.ds(pl.multiple_of(x * share, 16), share)
    pnr[x] = pn[own_classes, :]
    for b in range(blocks):
        here = slice(b * TILE, (b + 1) * TILE)
        total = pnr[0, :, here].astype(F32)
        for o in range(1, n_feat):
            total = total + pnr[o, :, here].astype(F32)
        pb[b] = total.astype(BF16)

    def scores(d):
        to = lax.rem(g + d, n_graph)
        return send(psend.at[to], parr.at[g], sem_a_s.at[d], sem_a_r.at[d], {"graph": to})

    def post(k):
        d = spread_order(k, n_graph)
        to = lax.rem(g + d, n_graph)
        for s in range(tpo):
            psend[to, :, s * TILE : (s + 1) * TILE] = pb[req_s[to, 0, s]]
        scores(d).start()

    loop(1, n_graph, post)
    for s in range(tpo):
        parr[g, :, s * TILE : (s + 1) * TILE] = pb[req_s[g, 0, s]]

    core_send.wait_recv()
    for i in range(n_dp):
        grad[core, i] = grad[core, i] + cr[i].astype(F32)
        ys[i] = grad[core, i].astype(BF16)

    def over_y(d):
        to = lax.rem(y + d, n_dp)
        return send(ys.at[to], yr.at[y], sem_y_s.at[d], sem_y_r.at[d], {"dp": to})

    for d in range(1, n_dp):
        over_y(d).start()

    for d in range(1, n_feat):
        scatter(d, 1).wait_recv()

    for d in range(1, n_dp):
        over_y(d).wait_recv()
    total = grad[core, y]
    for d in range(1, n_dp):
        total = total + yr[lax.rem(y + d, n_dp)].astype(F32)
    low = total.astype(BF16)
    top = n_feat * strip
    xs[...] = low[:top]
    tz[top : top + share, :] = low[top:]
    tz[top + share :, :] = jnp.zeros((tz.shape[0] - top - share, hidden), BF16)

    def over_x(d):
        to = lax.rem(x + d, n_feat)
        return send(
            xs.at[pl.ds(pl.multiple_of(to * strip, 16), strip), :],
            tz.at[pl.ds(pl.multiple_of(x * strip, 16), strip), :],
            sem_x_s.at[d],
            sem_x_r.at[d],
            {"feat": to},
        )

    for d in range(1, n_feat):
        over_x(d).start()
    own_strip = pl.ds(pl.multiple_of(x * strip, 16), strip)
    tz[own_strip, :] = xs[own_strip, :]
    for d in range(1, n_feat):
        over_x(d).wait_recv()

    piece = tz.shape[0] // n_z

    def rows_of(o):
        return pl.ds(pl.multiple_of(o * piece, 16), piece)

    def over_z(d):
        to = lax.rem(z + d, n_z)
        return send(tz.at[rows_of(to), :], zr.at[z], sem_z_s.at[d], sem_z_r.at[d], {"graph": to * 2 + core})

    loop(1, n_z, lambda d: over_z(d).start())

    acc[...] = dot_nt(parr[g], adj[:, lanes(g * pair, pair)])

    def arrive(k):
        d = spread_order(n_graph - k, n_graph)
        scores(d).wait_recv()
        o = lax.rem(g + n_graph - d, n_graph)
        acc[...] += dot_nt(parr[o], adj[:, lanes(o * pair, pair)])

    loop(1, n_graph, arrive)

    psr[x] = ps[own_classes, :]
    for b in range(blocks):
        here = slice(b * TILE, (b + 1) * TILE)
        total = psr[0, :, here].astype(F32)
        for o in range(1, n_feat):
            total = total + psr[o, :, here].astype(F32)
        if b < row_blocks:
            total = total + acc[:, here] * inv_v[0:1, here]
        lt[own_classes, here] = total.astype(BF16)
    gather_l = RingGather(lt, share, nodes, sem_l_s, sem_l_r, x, n_feat)
    gather_l.start()

    loop(1, n_z, lambda d: over_z(d).wait_recv())
    total = tz[rows_of(z), :].astype(F32)
    for d in range(1, n_z):
        total = total + zr[lax.rem(z + d, n_z)].astype(F32)
    fin[core, y, rows_of(z), :] = total.astype(BF16)

    def spread_z(d):
        part = fin.at[core, y, rows_of(z), :]
        return send(part, part, sem_zg_s.at[d], sem_zg_r.at[d], {"graph": lax.rem(z + d, n_z) * 2 + core})

    loop(1, n_z, lambda d: spread_z(d).start())
    gather_l.middle()
    loop(1, n_z, lambda d: spread_z(d).wait_recv())

    def spread_y(d):
        part = fin.at[core, y]
        return send(part, part, sem_yg_s.at[d], sem_yg_r.at[d], {"dp": lax.rem(y + d, n_dp)})

    def spread_core(d):
        part = fin.at[core, lax.rem(y + n_dp - d, n_dp)]
        return send(part, part, sem_cg_s.at[d], sem_cg_r.at[d], {"graph": sibling})

    for d in range(1, n_dp):
        spread_y(d).start()
    spread_core(0).start()
    gather_l.finish()
    eye_n = identity(TILE)

    def turn(b):
        t = dot_nt(eye_n, lt[:, lanes(b * TILE, TILE)])
        logits_o[pl.ds(pl.multiple_of(b * TILE, TILE), TILE), :] = t[:, :classes]

    loop(0, blocks, turn)
    for d in range(1, n_dp):
        spread_y(d).wait_recv()
        spread_core(d).start()
    for d in range(n_dp):
        spread_core(d).wait_recv()

    for k, first, second in ((0, g1s_o, g2s_o), (1, g1n_o, g2n_o)):
        for i in range(n_dp):
            for o in range(n_feat):
                first[i * strip : (i + 1) * strip, o * hidden : (o + 1) * hidden] = fin[
                    k, i, o * strip : (o + 1) * strip, :
                ].astype(F32)
        stacked = jnp.concatenate([fin[k, i, top : top + share, :] for i in range(n_dp)], axis=0)
        second[...] = dot_nt(eye, stacked)[:, :classes]

    core_send.wait_send()
    for d in range(1, n_feat):
        scatter(d, 0).wait_send()
        scatter(d, 1).wait_send()
        over_x(d).wait_send()
    for d in range(1, n_dp):
        over_y(d).wait_send()
        spread_y(d).wait_send()
    for d in range(n_dp):
        spread_core(d).wait_send()

    loop(1, n_graph, lambda d: scores(d).wait_send())

    def settle(d):
        over_z(d).wait_send()
        spread_z(d).wait_send()

    loop(1, n_z, settle)


def update(n_graph, n_feat, n_dp, rows, counts, requested, feat_t, ax_t, q_t, dl_t, inv, w1s, w1n, w2s, w2n, bits, classes):
    nodes, n_rows = feat_t.shape[1], ax_t.shape[1]
    width = feat_t.shape[0] // n_feat
    hidden = w1s.shape[1]
    n_slots, tpo = bits.shape[0], rows.shape[1]
    share = CPAD // n_feat
    strip = width // n_dp
    n_z = n_graph // 2
    held = n_feat * strip + share
    padded = -(-held // (16 * n_z)) * 16 * n_z
    vmem = pl.BlockSpec(memory_space=pltpu.VMEM)
    smem = pl.BlockSpec(memory_space=pltpu.SMEM)
    dma = pltpu.SemaphoreType.DMA
    blocks = nodes // TILE
    return pl.pallas_call(
        functools.partial(update_kernel, n_graph, n_feat, n_dp),
        out_shape=(
            jax.ShapeDtypeStruct((nodes, classes), F32),
            jax.ShapeDtypeStruct((width, n_feat * hidden), F32),
            jax.ShapeDtypeStruct((width, n_feat * hidden), F32),
            jax.ShapeDtypeStruct((hidden, classes), F32),
            jax.ShapeDtypeStruct((hidden, classes), F32),
        ),
        in_specs=[smem] * 3 + [vmem] * 10,
        out_specs=(vmem,) * 5,
        scratch_shapes=[
            pltpu.VMEM((hidden, n_feat * width), BF16),
            pltpu.VMEM((hidden, n_feat * width), BF16),
            pltpu.VMEM((CPAD, hidden), BF16),
            pltpu.VMEM((CPAD, hidden), BF16),
            pltpu.VMEM((hidden, nodes), BF16),
            pltpu.VMEM((hidden, nodes), BF16),
            pltpu.VMEM((CPAD, nodes), BF16),
            pltpu.VMEM((CPAD, nodes), BF16),
            pltpu.VMEM((n_feat, share, nodes), BF16),
            pltpu.VMEM((n_feat, share, nodes), BF16),
            pltpu.VMEM((blocks, share, TILE), BF16),
            pltpu.VMEM((n_graph, share, tpo * TILE), BF16),
            pltpu.VMEM((n_graph, share, tpo * TILE), BF16),
            pltpu.VMEM((n_rows, n_slots * TILE), BF16),
            pltpu.VMEM((8, TILE), BF16),
            pltpu.VMEM((share, n_rows), F32),
            pltpu.VMEM((CPAD, nodes), BF16),
            pltpu.VMEM((2, n_dp, held, hidden), F32),
            pltpu.VMEM((n_dp, held, hidden), BF16),
            pltpu.VMEM((n_dp, held, hidden), BF16),
            pltpu.VMEM((n_dp, held, hidden), BF16),
            pltpu.VMEM((n_dp, held, hidden), BF16),
            pltpu.VMEM((n_feat * strip, hidden), BF16),
            pltpu.VMEM((padded, hidden), BF16),
            pltpu.VMEM((n_z, padded // n_z, hidden), BF16),
            pltpu.VMEM((2, n_dp, padded, hidden), BF16),
            dma((2, n_feat)),
            dma((2, n_feat)),
            dma((n_graph,)),
            dma((n_graph,)),
            dma((4,)),
            dma((4,)),
            dma,
            dma,
            dma((n_dp,)),
            dma((n_dp,)),
            dma((n_feat,)),
            dma((n_feat,)),
            dma((n_z,)),
            dma((n_z,)),
            dma((n_z,)),
            dma((n_z,)),
            dma((n_dp,)),
            dma((n_dp,)),
            dma((n_dp,)),
            dma((n_dp,)),
        ],
        compiler_params=pltpu.CompilerParams(
            collective_id=1, has_side_effects=True, vmem_limit_bytes=58 * 1024 * 1024
        ),
    )(rows, counts, requested, feat_t, ax_t, q_t, dl_t, inv, w1s, w1n, w2s, w2n, bits)


def on_device(
    n_graph,
    n_feat,
    n_dp,
    features,
    w1_self,
    w1_neigh,
    w2_self,
    w2_neigh,
    tile_rows,
    tile_cols,
    tile_count,
    tile_bits,
    d_logits,
):
    feats = features[0]
    rows, cols, counts = tile_rows[0, 0], tile_cols[0, 0], tile_count[0, 0]
    bits = tile_bits[0, 0].reshape(-1, TILE, TILE)
    classes = d_logits.shape[2]
    dl_t = jnp.pad(d_logits[0].T, ((0, CPAD - classes), (0, 0)))

    feat_t, ax_t, q_t, inv, requested, w1s, w1n = exchange(
        n_graph, n_feat, rows, counts, cols, feats, dl_t, bits, w1_self, w1_neigh
    )
    w2s = jnp.pad(w2_self, ((0, 0), (0, CPAD - classes)))
    w2n = jnp.pad(w2_neigh, ((0, 0), (0, CPAD - classes)))
    logits, g1s, g1n, g2s, g2n = update(
        n_graph, n_feat, n_dp, rows, counts, requested, feat_t, ax_t, q_t, dl_t, inv, w1s, w1n, w2s, w2n, bits, classes
    )
    return logits[None], g1s, g1n, g2s, g2n


def solution(mesh):
    placed = (
        P("dp", "graph", "feat"),
        P("feat", None),
        P("feat", None),
        P("feat", None),
        P("feat", None),
        P("dp", "graph", None, None),
        P("dp", "graph", None, None),
        P("dp", "graph", None),
        P("dp", "graph", None, None, None, None),
        P("dp", "graph", None),
    )
    return jax.shard_map(
        functools.partial(on_device, mesh.shape["graph"], mesh.shape["feat"], mesh.shape["dp"]),
        mesh=mesh,
        in_specs=placed,
        out_specs=(
            P("dp", "graph", None),
            P("feat", None),
            P("feat", None),
            P("feat", None),
            P("feat", None),
        ),
        check_vma=False,
    )
```

```python
import functools

import jax
import jax.numpy as jnp
from jax import lax
from jax.experimental import pallas as pl
from jax.experimental.pallas import tpu as pltpu
from jax.sharding import PartitionSpec as P

MESH = pl.DeviceIdType.MESH
TILE = 128
TPO = 3
CPAD = 192
PARTS = 2
BF16, F32, I32 = jnp.bfloat16, jnp.float32, jnp.int32
NT = (((1,), (1,)), ((), ()))


def dot(a, b):
    return jnp.dot(a, b, preferred_element_type=F32)


def dot_nt(a, b):
    return lax.dot_general(a, b, NT, preferred_element_type=F32)


def loop(lo, hi, body):
    def step(i, carry):
        body(i)
        return carry

    lax.fori_loop(lo, hi, step, 0)


def spread_order(k, n):
    return n // 2 + (k // 2) * (1 - 2 * (k % 2))


def lanes(start, size):
    return pl.ds(pl.multiple_of(start, TILE), size)


def rows_at(start, size):
    return pl.ds(pl.multiple_of(start, 16), size)


def identity(rows, cols):
    same = lax.broadcasted_iota(I32, (rows, cols), 0) == lax.broadcasted_iota(I32, (rows, cols), 1)
    return same.astype(F32).astype(BF16)


def remote(src, dst, ssem, rsem, to):
    return pltpu.make_async_remote_copy(
        src_ref=src, dst_ref=dst, send_sem=ssem, recv_sem=rsem, device_id=to, device_id_type=MESH
    )


class RingGather:
    def __init__(self, buf, base, stride, rows, ssem, rsem, x, nx, axis="feat"):
        self.buf, self.base, self.stride, self.rows, self.axis = buf, base, stride, rows, axis
        self.ssem, self.rsem, self.x, self.nx = ssem, rsem, x, nx
        self.cols = buf.shape[1]

    def copy(self, owner, first, count, which, to):
        part = self.buf.at[rows_at(self.base + owner * self.stride, self.rows), pl.ds(first, count)]
        return remote(part, part, self.ssem.at[which], self.rsem.at[which], {self.axis: to})

    def parts(self):
        x, nx, c = self.x, self.nx, self.cols
        right, left = lax.rem(x + 1, nx), lax.rem(x + nx - 1, nx)
        return (
            self.copy(x, 0, c, 0, right),
            self.copy(x, 0, c, 1, left),
            self.copy(left, 0, c // 2, 2, right),
            self.copy(right, c // 2, c // 2, 3, left),
        )

    def start(self):
        a, b, _, _ = self.parts()
        a.start()
        b.start()

    def middle(self):
        a, b, c, d = self.parts()
        a.wait_recv()
        c.start()
        b.wait_recv()
        d.start()

    def arrive(self):
        _, _, c, d = self.parts()
        c.wait_recv()
        d.wait_recv()

    def settle(self):
        for p in self.parts():
            p.wait_send()


def step_kernel(
    n_graph,
    n_feat,
    n_dp,
    rows_s,
    count_s,
    cols_v,
    feat_v,
    dl_v,
    w2s_v,
    w2n_v,
    bits_h,
    w1s_h,
    w1n_h,
    lt,
    first_o,
    second_o,
    fin,
    bits,
    featb,
    featf,
    axf,
    send,
    arr,
    adj,
    acc,
    deg,
    dinv,
    qsend,
    qarr,
    cols_w,
    req_v,
    req_s,
    w1f,
    w1t,
    w2t,
    w2c,
    dq,
    pre,
    hid,
    dpre,
    pp,
    pr,
    pb,
    psend,
    parr,
    pacc,
    grad,
    cr,
    ys,
    yr,
    xs,
    tz,
    zr,
    sem_local,
    sem_req_s,
    sem_req_r,
    sem_f_s,
    sem_f_r,
    sem_q_s,
    sem_q_r,
    sem_w_s,
    sem_w_r,
    sem_g_s,
    sem_g_r,
    sem_p_s,
    sem_p_r,
    sem_a_s,
    sem_a_r,
    sem_c_s,
    sem_c_r,
    sem_y_s,
    sem_y_r,
    sem_x_s,
    sem_x_r,
    sem_z_s,
    sem_z_r,
    sem_zg_s,
    sem_zg_r,
    sem_yg_s,
    sem_yg_r,
    sem_cg_s,
    sem_cg_r,
):
    g = lax.axis_index("graph")
    x = lax.axis_index("feat")
    y = lax.axis_index("dp")
    core = lax.rem(g, 2)
    z = g // 2
    n_z = n_graph // 2
    sibling = g + 1 - 2 * core
    width, nodes = feat_v.shape
    n_rows = adj.shape[0]
    row_blocks, blocks = n_rows // TILE, nodes // TILE
    hidden = hid.shape[0]
    share = CPAD // n_feat
    strip = width // n_dp
    pair = TPO * TILE
    part = width // PARTS
    own_rows = rows_at(x * width, width)

    barrier = pltpu.get_barrier_semaphore()

    def greet(d):
        pl.semaphore_signal(barrier, inc=1, device_id={"graph": lax.rem(g + d, n_graph)}, device_id_type=MESH)

    loop(1, n_graph, greet)
    for d in range(1, n_feat):
        pl.semaphore_signal(barrier, inc=1, device_id={"feat": lax.rem(x + d, n_feat)}, device_id_type=MESH)
    for d in range(1, n_dp):
        pl.semaphore_signal(barrier, inc=1, device_id={"dp": lax.rem(y + d, n_dp)}, device_id_type=MESH)

    load_bits = pltpu.make_async_copy(bits_h, bits, sem_local.at[0])
    load_bits.start()
    w1_src = (w1s_h, w1n_h)
    own_w1 = [
        pltpu.make_async_copy(w1_src[k].at[:, lanes(x * hidden, hidden)], w1f.at[k, own_rows, :], sem_local.at[1 + k])
        for k in range(2)
    ]
    for c in own_w1:
        c.start()
    featf[own_rows, :] = feat_v[...]
    for i in range(PARTS):
        for b in range(blocks):
            featb[i, b] = feat_v[i * part : (i + 1) * part, b * TILE : (b + 1) * TILE]
    cols_w[:, :, :n_graph] = cols_v[...]
    req_v[g] = cols_w[...]

    pl.semaphore_wait(barrier, n_graph - 1 + n_feat - 1 + n_dp - 1)

    def request(d):
        to = lax.rem(g + d, n_graph)
        return remote(cols_w, req_v.at[g], sem_req_s.at[d], sem_req_r.at[d], {"graph": to})

    loop(1, n_graph, lambda d: request(d).start())

    gather_feat = RingGather(featf, 0, width, width, sem_g_s.at[0], sem_g_r.at[0], x, n_feat)
    gather_q = RingGather(dq, CPAD, share, share, sem_g_s.at[1], sem_g_r.at[1], x, n_feat)
    gather_l = RingGather(lt, 0, share, share, sem_g_s.at[2], sem_g_r.at[2], x, n_feat)
    gather_ax = [
        RingGather(axf, i * part, width, part, sem_g_s.at[3 + i], sem_g_r.at[3 + i], x, n_feat) for i in range(PARTS)
    ]

    loop(1, n_graph, lambda d: request(d).wait_recv())
    fetch = pltpu.make_async_copy(req_v, req_s, sem_local.at[3])
    fetch.start()
    fetch.wait()

    def feats(i, d):
        to = lax.rem(g + d, n_graph)
        return remote(send.at[i, to], arr.at[i, g], sem_f_s.at[i, d], sem_f_r.at[i, d], {"graph": to})

    def pick(i, to, dst):
        for s in range(TPO):
            dst[i, to, :, s * TILE : (s + 1) * TILE] = featb[i, req_s[to, s, 0, g]]

    def post(i, k):
        d = spread_order(k, n_graph)
        to = lax.rem(g + d, n_graph)
        pick(i, to, send)
        feats(i, d).start()

    loop(1, n_graph, lambda k: post(0, k))
    gather_feat.start()
    for i in range(PARTS):
        pick(i, g, arr)

    def weights(d, k):
        to = lax.rem(x + d, n_feat)
        return remote(
            w1_src[k].at[:, lanes(to * hidden, hidden)],
            w1f.at[k, own_rows, :],
            sem_w_s.at[k, d],
            sem_w_r.at[k, d],
            {"feat": to},
        )

    for k in range(2):
        for d in range(1, n_feat):
            weights(d, k).start()

    load_bits.wait()

    def build(o):
        for s in range(TPO):
            t = o * TPO + s
            on = (s < count_s[o]).astype(I32)
            tile = (bits[t] * on).astype(F32)
            row = rows_s[s, 0, o]
            for r in range(row_blocks):
                here = (row == r).astype(F32)
                adj[r * TILE : (r + 1) * TILE, lanes(t * TILE, TILE)] = (tile * here).astype(BF16)

    loop(0, n_graph, build)
    deg[...] = jnp.zeros(deg.shape, F32)

    def degree(o):
        deg[...] += dot_nt(jnp.ones((8, pair), BF16), adj[:, lanes(o * pair, pair)])

    loop(0, n_graph, degree)
    deg[...] = 1.0 / jnp.maximum(deg[...], 1.0)

    eye_c = identity(CPAD, dl_v.shape[0])
    quarter = nodes // 4

    def pad_classes(i):
        here = lanes(i * quarter, quarter)
        dq[:CPAD, here] = dot(eye_c, dl_v[:, here]).astype(BF16)

    loop(0, 4, pad_classes)
    w2t[:CPAD, :] = dot(eye_c, w2s_v[...]).astype(BF16)
    w2t[CPAD:, :] = dot(eye_c, w2n_v[...]).astype(BF16)
    eye = identity(hidden, hidden)
    w2c[...] = dot_nt(eye, w2t[...]).astype(BF16)

    own_d = dq[rows_at(x * share, share), :n_rows].astype(F32) * deg[0:1, :]
    for r in range(row_blocks):
        dinv[r] = own_d[:, r * TILE : (r + 1) * TILE].astype(BF16)

    def terms(o):
        for s in range(TPO):
            t = o * TPO + s
            on = (s < count_s[o]).astype(I32)
            tile = (bits[t] * on).astype(F32).astype(BF16)
            qsend[o, s] = dot(dinv[rows_s[s, 0, o]], tile).astype(BF16)

    loop(0, n_graph, terms)
    qarr[g, :TPO] = qsend[g]

    def blank(o):
        qarr[o, TPO] = jnp.zeros((share, TILE), BF16)

    loop(0, n_graph, blank)

    gather_feat.middle()
    for c in own_w1:
        c.wait()
    for k in range(2):
        for d in range(1, n_feat):
            weights(d, k).wait_recv()
        w1t[k] = dot_nt(eye, w1f[k]).astype(BF16)

    def q_terms(d):
        to = lax.rem(g + d, n_graph)
        return remote(qsend.at[to], qarr.at[g, pl.ds(0, TPO)], sem_q_s.at[d], sem_q_r.at[d], {"graph": to})

    for i in range(PARTS):
        acc[...] = dot_nt(arr[i, g], adj[:, lanes(g * pair, pair)])

        def arrive(k, i=i):
            d = spread_order(k, n_graph)
            feats(i, d).wait_recv()
            if i < PARTS - 1:
                post(i + 1, k)
            o = lax.rem(g + n_graph - d, n_graph)
            acc[...] += dot_nt(arr[i, o], adj[:, lanes(o * pair, pair)])

        loop(1, n_graph // 2, arrive)
        if i > 0:
            gather_ax[i - 1].middle()
        if i == PARTS - 1:
            loop(1, n_graph, lambda d: q_terms(d).start())
        loop(n_graph // 2, n_graph, arrive)
        axf[rows_at(x * width + i * part, part), :] = (acc[...] * deg[0:1, :]).astype(BF16)
        gather_ax[i].start()
        if i == 0:
            gather_feat.arrive()

            def own_layer(n):
                here = lanes(n * quarter, quarter)
                pre[:, here] = dot(w1t[0], featf[:, here])

            loop(0, 4, own_layer)

    own_q = rows_at(CPAD + x * share, share)
    gather_ax[PARTS - 1].middle()
    loop(1, n_graph, lambda d: q_terms(d).wait_recv())

    def column(c):
        total = jnp.zeros((share, TILE), F32)
        for o in range(n_graph):
            which = jnp.where(
                req_s[o, 0, 0, g] == c, 0, jnp.where(req_s[o, 1, 0, g] == c, 1, jnp.where(req_s[o, 2, 0, g] == c, 2, TPO))
            )
            total = total + qarr[o, which].astype(F32)
        dq[own_q, lanes(c * TILE, TILE)] = total.astype(BF16)

    loop(0, blocks, column)
    gather_q.start()

    for i in range(PARTS):
        gather_ax[i].arrive()

    def layer(n, with_neighbours):
        here = lanes(n * quarter, quarter)
        v = pre[:, here]
        if with_neighbours:
            v = v + dot(w1t[1], axf[:, here])
        sig = 1.0 / (1.0 + jnp.exp(-v))
        act = (v * sig).astype(BF16)
        hid[:, here] = act
        pp[:, here] = dot(w2t[...], act).astype(BF16)
        pre[:, here] = sig * (1.0 + v * (1.0 - sig))

    loop(0, 3, lambda n: layer(n, True))
    layer(3, False)

    def scatter(d, k):
        to = lax.rem(x + d, n_feat)
        return remote(
            pp.at[rows_at(k * CPAD + to * share, share), :],
            pr.at[k, x],
            sem_p_s.at[k, d],
            sem_p_r.at[k, d],
            {"feat": to},
        )

    gather_q.middle()
    for d in range(1, n_feat):
        scatter(d, 1).start()

    gather_q.arrive()

    def backward(n):
        here = lanes(n * quarter, quarter)
        dpre[:, here] = (dot(w2c[...], dq[:, here]) * pre[:, here]).astype(BF16)

    loop(0, 4, backward)
    top = n_feat * strip

    def gradients(k):
        src, cols = ((featf, nodes), (axf, n_rows))[k]
        dp = dpre[:, :cols]

        t = dot_nt(src[...], dp)
        for o in range(n_feat):
            for i in range(n_dp):
                at = o * width + i * strip
                grad[k, i, o * strip : (o + 1) * strip, :] = t[at : at + strip]
        t = dot_nt(dq[k * CPAD : (k + 1) * CPAD, :], hid[...])
        for i in range(n_dp):
            grad[k, i, top:, :] = t[i * share : (i + 1) * share]

    gradients(0)
    gradients(1)
    core_send = remote(grad.at[1 - core], cr, sem_c_s, sem_c_r, {"graph": sibling})
    core_send.start()

    def score_sum(k, b):
        here = slice(b * TILE, (b + 1) * TILE)
        total = pr[k, 0, :, here].astype(F32)
        for o in range(1, n_feat):
            total = total + pr[k, o, :, here].astype(F32)
        return total

    for d in range(1, n_feat):
        scatter(d, 1).wait_recv()
    pr[1, x] = pp[rows_at(CPAD + x * share, share), :]
    pr[0, x] = pp[rows_at(x * share, share), :]
    for b in range(blocks):
        pb[b] = score_sum(1, b).astype(BF16)

    def scores(d):
        to = lax.rem(g + d, n_graph)
        return remote(psend.at[to], parr.at[g], sem_a_s.at[d], sem_a_r.at[d], {"graph": to})

    def pick_scores(to, dst):
        for s in range(TPO):
            dst[to, :, s * TILE : (s + 1) * TILE] = pb[req_s[to, s, 0, g]]

    def post_scores(k):
        d = spread_order(k, n_graph)
        to = lax.rem(g + d, n_graph)
        pick_scores(to, psend)
        scores(d).start()

    loop(1, n_graph, post_scores)
    pick_scores(g, parr)
    for d in range(1, n_feat):
        scatter(d, 0).start()

    core_send.wait_recv()
    for i in range(n_dp):
        total = grad[core, i] + cr[i]
        grad[core, i] = total
        ys[i] = total.astype(BF16)

    def over_y(d):
        to = lax.rem(y + d, n_dp)
        return remote(ys.at[to], yr.at[y], sem_y_s.at[d], sem_y_r.at[d], {"dp": to})

    for d in range(1, n_dp):
        over_y(d).start()

    for d in range(1, n_dp):
        over_y(d).wait_recv()
    total = grad[core, y]
    for d in range(1, n_dp):
        total = total + yr[lax.rem(y + d, n_dp)].astype(F32)
    xs[...] = total
    tz[top : top + share, :] = total[top:]
    tz[top + share :, :] = jnp.zeros((tz.shape[0] - top - share, hidden), F32)

    def over_x(d):
        to = lax.rem(x + d, n_feat)
        return remote(
            xs.at[rows_at(to * strip, strip), :],
            tz.at[rows_at(x * strip, strip), :],
            sem_x_s.at[d],
            sem_x_r.at[d],
            {"feat": to},
        )

    for d in range(1, n_feat):
        over_x(d).start()
    own_strip = rows_at(x * strip, strip)
    tz[own_strip, :] = xs[own_strip, :]
    for d in range(1, n_feat):
        over_x(d).wait_recv()

    piece = tz.shape[0] // n_z

    def over_z(d):
        to = lax.rem(z + d, n_z)
        return remote(
            tz.at[rows_at(to * piece, piece), :], zr.at[z], sem_z_s.at[d], sem_z_r.at[d], {"graph": to * 2 + core}
        )

    loop(1, n_z, lambda d: over_z(d).start())

    pacc[...] = dot_nt(parr[g], adj[:, lanes(g * pair, pair)])

    def arrive_scores(k):
        d = spread_order(n_graph - k, n_graph)
        scores(d).wait_recv()
        o = lax.rem(g + n_graph - d, n_graph)
        pacc[...] += dot_nt(parr[o], adj[:, lanes(o * pair, pair)])

    loop(1, n_graph, arrive_scores)
    for d in range(1, n_feat):
        scatter(d, 0).wait_recv()
    own_classes = rows_at(x * share, share)
    for b in range(blocks):
        here = slice(b * TILE, (b + 1) * TILE)
        total = score_sum(0, b)
        if b < row_blocks:
            total = total + pacc[:, here] * deg[0:1, here]
        lt[own_classes, here] = total.astype(BF16)
    gather_l.start()

    loop(1, n_z, lambda d: over_z(d).wait_recv())
    own_piece = rows_at(z * piece, piece)
    total = tz[own_piece, :]
    for d in range(1, n_z):
        total = total + zr[lax.rem(z + d, n_z)]
    held = tz.shape[0]

    def held_rows(owner):
        return (core * n_dp + owner) * held

    own_fin = rows_at(held_rows(y) + z * piece, piece)
    fin[own_fin, :] = total.astype(BF16)

    def spread_z(d):
        mine = fin.at[own_fin, :]
        return remote(mine, mine, sem_zg_s.at[d], sem_zg_r.at[d], {"graph": lax.rem(z + d, n_z) * 2 + core})

    loop(1, n_z, lambda d: spread_z(d).start())
    loop(1, n_z, lambda d: spread_z(d).wait_recv())
    gather_l.middle()

    gather_y = RingGather(fin, core * n_dp * held, held, held, sem_yg_s, sem_yg_r, y, n_dp, "dp")

    def spread_core(d):
        rows = fin.at[rows_at(held_rows(lax.rem(y + d, n_dp)), held), :]
        return remote(rows, rows, sem_cg_s.at[d], sem_cg_r.at[d], {"graph": sibling})

    gather_y.start()
    spread_core(0).start()
    gather_y.middle()
    spread_core(1).start()
    spread_core(n_dp - 1).start()
    gather_y.arrive()
    spread_core(2).start()
    gather_l.arrive()
    for d in range(n_dp):
        spread_core(d).wait_recv()

    for k in range(2):
        for i in range(n_dp):
            base = (k * n_dp + i) * held
            for o in range(n_feat):
                first_o[k, i * strip : (i + 1) * strip, o * hidden : (o + 1) * hidden] = fin[
                    base + o * strip : base + (o + 1) * strip, :
                ]
            second_o[k, i * share : (i + 1) * share, :] = fin[base + top : base + top + share, :]

    def settle(d):
        request(d).wait_send()
        q_terms(d).wait_send()
        scores(d).wait_send()
        for i in range(PARTS):
            feats(i, d).wait_send()

    loop(1, n_graph, settle)

    def settle_z(d):
        over_z(d).wait_send()
        spread_z(d).wait_send()

    loop(1, n_z, settle_z)
    core_send.wait_send()
    for d in range(1, n_feat):
        for k in range(2):
            weights(d, k).wait_send()
            scatter(d, k).wait_send()
        over_x(d).wait_send()
    for d in range(1, n_dp):
        over_y(d).wait_send()
    for d in range(n_dp):
        spread_core(d).wait_send()
    for ring in (gather_feat, gather_q, gather_l, gather_y, *gather_ax):
        ring.settle()


def fused_step(n_graph, n_feat, n_dp, rows, counts, cols, feat_t, dl_t, w2s_t, w2n_t, bits, w1s, w1n):
    width, nodes = feat_t.shape
    n_rows = nodes // 4 * 3
    n_slots, blocks = bits.shape[0], nodes // TILE
    hidden = w2s_t.shape[1]
    share = CPAD // n_feat
    strip = width // n_dp
    n_z = n_graph // 2
    held = n_feat * strip + share
    padded = -(-held // (16 * n_z)) * 16 * n_z
    part = width // PARTS
    pair = TPO * TILE
    vmem = pl.BlockSpec(memory_space=pltpu.VMEM)
    smem = pl.BlockSpec(memory_space=pltpu.SMEM)
    hbm = pl.BlockSpec(memory_space=pl.ANY)
    dma = pltpu.SemaphoreType.DMA
    return pl.pallas_call(
        functools.partial(step_kernel, n_graph, n_feat, n_dp),
        out_shape=(
            jax.ShapeDtypeStruct((CPAD, nodes), BF16),
            jax.ShapeDtypeStruct((2, width, n_feat * hidden), BF16),
            jax.ShapeDtypeStruct((2, CPAD, hidden), BF16),
        ),
        in_specs=[smem] * 2 + [vmem] * 5 + [hbm] * 3,
        out_specs=(vmem,) * 3,
        scratch_shapes=[
            pltpu.VMEM((2 * n_dp * padded, hidden), BF16),
            pltpu.VMEM((n_slots, TILE, TILE), I32),
            pltpu.VMEM((PARTS, blocks, part, TILE), BF16),
            pltpu.VMEM((n_feat * width, nodes), BF16),
            pltpu.VMEM((n_feat * width, n_rows), BF16),
            pltpu.VMEM((PARTS, n_graph, part, pair), BF16),
            pltpu.VMEM((PARTS, n_graph, part, pair), BF16),
            pltpu.VMEM((n_rows, n_slots * TILE), BF16),
            pltpu.VMEM((part, n_rows), F32),
            pltpu.VMEM((8, n_rows), F32),
            pltpu.VMEM((n_rows // TILE, share, TILE), BF16),
            pltpu.VMEM((n_graph, TPO, share, TILE), BF16),
            pltpu.VMEM((n_graph, TPO + 1, share, TILE), BF16),
            pltpu.VMEM((TPO, 1, TILE), I32),
            pltpu.VMEM((n_graph, TPO, 1, TILE), I32),
            pltpu.SMEM((n_graph, TPO, 1, TILE), I32),
            pltpu.VMEM((2, n_feat * width, hidden), BF16),
            pltpu.VMEM((2, hidden, n_feat * width), BF16),
            pltpu.VMEM((2 * CPAD, hidden), BF16),
            pltpu.VMEM((hidden, 2 * CPAD), BF16),
            pltpu.VMEM((2 * CPAD, nodes), BF16),
            pltpu.VMEM((hidden, nodes), F32),
            pltpu.VMEM((hidden, nodes), BF16),
            pltpu.VMEM((hidden, nodes), BF16),
            pltpu.VMEM((2 * CPAD, nodes), BF16),
            pltpu.VMEM((2, n_feat, share, nodes), BF16),
            pltpu.VMEM((blocks, share, TILE), BF16),
            pltpu.VMEM((n_graph, share, pair), BF16),
            pltpu.VMEM((n_graph, share, pair), BF16),
            pltpu.VMEM((share, n_rows), F32),
            pltpu.VMEM((2, n_dp, held, hidden), F32),
            pltpu.VMEM((n_dp, held, hidden), F32),
            pltpu.VMEM((n_dp, held, hidden), BF16),
            pltpu.VMEM((n_dp, held, hidden), BF16),
            pltpu.VMEM((held, hidden), F32),
            pltpu.VMEM((padded, hidden), F32),
            pltpu.VMEM((n_z, padded // n_z, hidden), F32),
            dma((4,)),
            dma((n_graph,)),
            dma((n_graph,)),
            dma((PARTS, n_graph)),
            dma((PARTS, n_graph)),
            dma((n_graph,)),
            dma((n_graph,)),
            dma((2, n_feat)),
            dma((2, n_feat)),
            dma((3 + PARTS, 4)),
            dma((3 + PARTS, 4)),
            dma((2, n_feat)),
            dma((2, n_feat)),
            dma((n_graph,)),
            dma((n_graph,)),
            dma,
            dma,
            dma((n_dp,)),
            dma((n_dp,)),
            dma((n_feat,)),
            dma((n_feat,)),
            dma((n_z,)),
            dma((n_z,)),
            dma((n_z,)),
            dma((n_z,)),
            dma((n_dp,)),
            dma((n_dp,)),
            dma((n_dp,)),
            dma((n_dp,)),
        ],
        compiler_params=pltpu.CompilerParams(
            collective_id=0, has_side_effects=True, vmem_limit_bytes=60 * 1024 * 1024
        ),
    )(rows, counts, cols, feat_t, dl_t, w2s_t, w2n_t, bits, w1s, w1n)


def on_device(
    n_graph,
    n_feat,
    n_dp,
    features,
    w1_self,
    w1_neigh,
    w2_self,
    w2_neigh,
    tile_rows,
    tile_cols,
    tile_count,
    tile_bits,
    d_logits,
):
    classes = d_logits.shape[2]
    lt, first, second = fused_step(
        n_graph,
        n_feat,
        n_dp,
        tile_rows[0, 0].T[:, None],
        tile_count[0, 0],
        tile_cols[0, 0].T[:, None],
        features[0].T,
        d_logits[0].T,
        w2_self.T,
        w2_neigh.T,
        tile_bits[0, 0].reshape(-1, TILE, TILE),
        w1_self,
        w1_neigh,
    )
    logits = lt[:classes].astype(F32).T
    first, second = first.astype(F32), second[:, :classes].astype(F32)
    return logits[None], first[0], first[1], second[0].T, second[1].T


def solution(mesh):
    placed = (
        P("dp", "graph", "feat"),
        P("feat", None),
        P("feat", None),
        P("feat", None),
        P("feat", None),
        P("dp", "graph", None, None),
        P("dp", "graph", None, None),
        P("dp", "graph", None),
        P("dp", "graph", None, None, None, None),
        P("dp", "graph", None),
    )
    return jax.shard_map(
        functools.partial(on_device, mesh.shape["graph"], mesh.shape["feat"], mesh.shape["dp"]),
        mesh=mesh,
        in_specs=placed,
        out_specs=(
            P("dp", "graph", None),
            P("feat", None),
            P("feat", None),
            P("feat", None),
            P("feat", None),
        ),
        check_vma=False,
    )
```
